256 devices in a mesh: row: 16 (over y, x), col: 16 (over z, core).
Axes of the slice: x: 4, y: 4, z: 8, core: 2. Of those that a mesh axis runs over, the one named last changes fastest.
Arguments:
- rhs_one: bfloat16 [16, 16, 2, 256, 512], P('row', 'col'), may hold values from -6 to 6
- inv_one: bfloat16 [16, 16, 2, 256, 256], P('row', 'col'), as said below
- rhs_two: bfloat16 [16, 16, 1, 256, 512], P('row', 'col'), may hold values from -6 to 6
- inv_two: bfloat16 [16, 16, 1, 256, 256], P('row', 'col'), as said below
- blocks: bfloat16 [16, 16, 80, 256, 256], P('row', 'col'), may hold values from -0.0390625 to 0.0390625
- block_rows: int32 [16, 16, 80], P('row', 'col'), may hold values from 0 to 15
- block_cols: int32 [16, 16, 80], P('row', 'col'), may hold values from 0 to 31
Outputs:
- solved_one: bfloat16 [16, 16, 2, 256, 512], P('row', 'col')
- solved_two: bfloat16 [16, 16, 1, 256, 512], P('row', 'col')
The draws below stay inside these ranges and needn't reach their ends.
Inputs may be any that keep to these rules, and one draw needn't show every extreme that they name: `inv_one`: each 256 by 256 block is lower triangular with diagonal entries from 0.5 to 1.5. `inv_two`: each 256 by 256 block is lower triangular with diagonal entries from 0.5 to 1.5.
All inputs are finite; a program needn't handle non-finite values.
Results may differ from the reference program's by a relative error of at most 0.0055.
Values may be sent and summed in bfloat16 or wider, within the bound.
No kernel may reach another device: no remote copies, remote signals or barrier semaphores. Data moves between devices by JAX's collectives and lax.ppermute only.
A program may use at most 128 MiB of HBM per device.

```python
import jax
import jax.numpy as jnp
from jax import lax

W = 256
R = 512
Q1 = 2
Q2 = 1
NB = 80
N_ROW = 16
N_COL = 16


def shape_triangle(spread, key, order_value):
    row_index = lax.broadcasted_iota(jnp.int32, spread.shape, spread.ndim - 2)
    col_index = lax.broadcasted_iota(jnp.int32, spread.shape, spread.ndim - 1)
    pivots = jax.random.uniform(key, spread.shape[:-1], jnp.float32, 0.5, 1.5)
    strict_part = jnp.where(row_index > col_index, spread * order_value ** (-0.5), 0.0)
    return (strict_part + jnp.where(row_index == col_index, pivots[..., None], 0.0)).astype(jnp.bfloat16)


def draw_inv_one(key, part):
    key = jax.random.fold_in(key, 11)
    first, second = jax.random.split(key)
    shape = (N_ROW, N_COL, Q1, W, W)
    spread = jax.random.normal(first, shape, jnp.float32)
    return shape_triangle(spread, second, W)


def draw_inv_two(key, part):
    key = jax.random.fold_in(key, 23)
    first, second = jax.random.split(key)
    shape = (N_ROW, N_COL, Q2, W, W)
    spread = jax.random.normal(first, shape, jnp.float32)
    return shape_triangle(spread, second, W)


def with_ends(array, key, smallest, top_value):
    index_at = [jax.random.randint(jax.random.fold_in(key, axis), (), 0, length) for axis, length in enumerate(array.shape)]
    longest = array.shape.index(max(array.shape))
    beside = index_at[:longest] + [(index_at[longest] + 1) % array.shape[longest]] + index_at[longest + 1:]
    return array.at[tuple(index_at)].set(smallest).at[tuple(beside)].set(top_value)


def level_of(stream_key, dims, cuts, least, top_value):
    factor_of, own = 1.0, jax.random.fold_in(stream_key, 6)
    for axis_at, shards_of in cuts:
        draws = jnp.exp(jax.random.uniform(jax.random.fold_in(own, axis_at), (shards_of,), jnp.float32, least / len(cuts), top_value / len(cuts)))
        factor_of = factor_of * jnp.repeat(draws, dims[axis_at] // shards_of).reshape([-1 if axis == axis_at else 1 for axis in range(len(dims))])
    return factor_of


def normal_values(key, extent, width, reach, cuts=(), kind=jnp.bfloat16):
    loudness = level_of(key, extent, cuts, -0.22, 0.18) if cuts else 1.0
    result = jax.random.normal(key, extent, jnp.float32) * width * loudness
    return jnp.minimum(jnp.maximum(result, -reach), reach).astype(kind)


def setup_inputs(seed: int = 0) -> dict:
    key_list = jax.random.split(jax.random.key(seed), 8)
    rhs_one = normal_values(key_list[0], (N_ROW, N_COL, Q1, W, R), 1.0, 6.0, ((0, 16), (1, 16)))
    inv_one = draw_inv_one(jax.random.fold_in(key_list[7], 71), 0)
    rhs_two = normal_values(key_list[2], (N_ROW, N_COL, Q2, W, R), 1.0, 6.0, ((0, 16), (1, 16)))
    inv_two = draw_inv_two(jax.random.fold_in(key_list[7], 71), 0)
    blocks = normal_values(key_list[4], (N_ROW, N_COL, NB, W, W), (W * NB // Q2) ** -0.5, 0.0390625, ((0, 16), (1, 16)))
    block_rows = with_ends(jax.random.randint(key_list[5], (N_ROW, N_COL, NB), 0, N_COL * Q2), jax.random.fold_in(key_list[5], 1), 0, (N_COL * Q2) - 1).astype(jnp.int32)
    block_cols = with_ends(jax.random.randint(key_list[6], (N_ROW, N_COL, NB), 0, N_ROW * Q1), jax.random.fold_in(key_list[6], 1), 0, (N_ROW * Q1) - 1).astype(jnp.int32)
    return dict(rhs_one=rhs_one, inv_one=inv_one, rhs_two=rhs_two, inv_two=inv_two, blocks=blocks, block_rows=block_rows, block_cols=block_cols)


def apply_inverse(inverse, values):
    return jnp.einsum("...vw,...wr->...vr", inverse.astype(jnp.float32), values.astype(jnp.float32), precision=lax.Precision.HIGHEST)


def reference(rhs_one, inv_one, rhs_two, inv_two, blocks, block_rows, block_cols):
    solved_one = lax.map(lambda bundle: apply_inverse(bundle[0], bundle[1]).astype(jnp.bfloat16), (inv_one, rhs_one))
    by_column = jnp.moveaxis(solved_one, 1, 0).reshape(N_COL, N_ROW * Q1, W, R)
    labels = jnp.arange(N_COL * Q2, dtype=jnp.int32)

    def device_term(running, bundle):
        factor, targets, sources, column = bundle
        picked = jnp.take(column, sources.astype(jnp.int32), axis=0).astype(jnp.float32)
        product = jnp.einsum("kvw,kwr->kvr", factor.astype(jnp.float32), picked, precision=lax.Precision.HIGHEST)
        selector = (targets[None, :] == labels[:, None]).astype(jnp.float32)
        return running + jnp.einsum("dk,kvr->dvr", selector, product, precision=lax.Precision.HIGHEST), None

    def row_solve(bundle):
        rhs_row, inv_row, factor_row, target_row, source_row = bundle
        initial = jnp.zeros((N_COL * Q2, W, R), jnp.float32)
        total, unused = lax.scan(device_term, initial, (factor_row, target_row, source_row, by_column))
        residual = (rhs_row.astype(jnp.float32) - total.reshape(N_COL, Q2, W, R)).astype(jnp.bfloat16)
        return apply_inverse(inv_row, residual).astype(jnp.bfloat16)

    solved_two = lax.map(row_solve, (rhs_two, inv_two, blocks, block_rows, block_cols))
    return (solved_one, solved_two)
```

```python
import functools

import jax
import jax.numpy as jnp
from jax import lax
from jax.experimental import pallas as pl
from jax.experimental.pallas import tpu as pltpu
from jax.sharding import PartitionSpec as P

WIDTHS = (512,)
STEP = 8
BOTH = ("row", "col")
VMEM_LIMIT = 48 * 1024 * 1024
F32 = jnp.float32
BF16 = jnp.bfloat16


def whole(memory=pltpu.VMEM):
    return pl.BlockSpec(memory_space=memory)


def shape(dims, dtype=BF16):
    return jax.ShapeDtypeStruct(dims, dtype)


def params():
    return pltpu.CompilerParams(vmem_limit_bytes=VMEM_LIMIT)


def ring_pairs(axis, steps):
    pairs = []
    for y in range(4):
        for x in range(4):
            for z in range(8):
                for core in range(2):
                    way = steps if core == 0 else -steps
                    to_y, to_x, to_z = y, x, z
                    if axis == "x":
                        to_x = (x + way) % 4
                    elif axis == "y":
                        to_y = (y + way) % 4
                    else:
                        to_z = (z + way) % 8
                    pairs.append(((y * 4 + x) * 16 + z * 2 + core, (to_y * 4 + to_x) * 16 + to_z * 2 + core))
    return pairs


def move(value, axis, steps):
    return lax.ppermute(value, BOTH, ring_pairs(axis, steps))


def swap_cores(value):
    return lax.ppermute(value, "col", [(i, i ^ 1) for i in range(16)])


def solve_one_kernel(widths, rhs, inverse, solved, *parts):
    for q in range(2):
        value = jnp.dot(inverse[q], rhs[q], preferred_element_type=F32).astype(BF16)
        solved[q] = value
        start = 0
        for i, width in enumerate(widths):
            parts[2 * i + q][0] = value[:, start : start + width]
            start += width


def solve_one(rhs, inverse, widths):
    outs = [shape(rhs.shape)]
    for width in widths:
        outs += [shape((1, rhs.shape[1], width))] * 2
    return pl.pallas_call(
        functools.partial(solve_one_kernel, widths),
        out_shape=outs,
        in_specs=[whole()] * 2,
        out_specs=[whole()] * len(outs),
        compiler_params=params(),
    )(rhs, inverse)


def couple_kernel(places, source_slot, target_slot, blocks, *refs):
    count = len(places)
    pieces = refs[:count]
    keep, send, sources, total, sems = refs[count:]
    step = pl.program_id(0)

    @pl.when(step == 0)
    def _():
        copies = []
        for i, (piece, (start, size)) in enumerate(zip(pieces, places)):
            copies.append(pltpu.make_async_copy(piece, sources.at[pl.ds(start, size)], sems.at[i]))
            copies[-1].start()
        total[...] = jnp.zeros_like(total)
        for copy in copies:
            copy.wait()

    for j in range(STEP):
        index = step * STEP + j
        product = jnp.dot(blocks[j], sources[source_slot[index]], preferred_element_type=F32)
        total[target_slot[index]] += product

    @pl.when(step == pl.num_programs(0) - 1)
    def _():
        keep[...] = total[:8]
        send[...] = total[8:].astype(BF16)


def couple(source_slot, target_slot, blocks, pieces, places):
    count, rows, _ = blocks.shape
    width = pieces[0].shape[-1]
    return pl.pallas_call(
        functools.partial(couple_kernel, places),
        out_shape=[shape((8, rows, width), F32), shape((8, rows, width))],
        grid_spec=pltpu.PrefetchScalarGridSpec(
            num_scalar_prefetch=2,
            grid=(count // STEP,),
            in_specs=[pl.BlockSpec((STEP, rows, rows), lambda i, *_: (i, 0, 0))] + [whole(pl.ANY)] * len(pieces),
            out_specs=[pl.BlockSpec((8, rows, width), lambda i, *_: (0, 0, 0))] * 2,
            scratch_shapes=[
                pltpu.VMEM((32, rows, width), BF16),
                pltpu.VMEM((16, rows, width), F32),
                pltpu.SemaphoreType.DMA((len(pieces),)),
            ],
        ),
        compiler_params=params(),
        cost_estimate=pl.CostEstimate(
            flops=2 * count * rows * rows * width, bytes_accessed=2 * count * rows * rows, transcendentals=0
        ),
    )(source_slot, target_slot, blocks, *pieces)


def first_kernel(keep, other, near_fwd, near_bwd, far_fwd, far_bwd, kept):
    def part(u):
        return keep[u] + other[u].astype(F32)

    near_fwd[0] = part(1).astype(BF16)
    near_fwd[1] = part(3).astype(BF16)
    near_bwd[0] = part(7).astype(BF16)
    near_bwd[1] = part(5).astype(BF16)
    half = far_fwd.shape[0]
    middle = part(4).astype(BF16)
    far_fwd[...] = middle[:half]
    far_bwd[...] = middle[half:]
    kept[0] = part(0)
    kept[1] = part(2)
    kept[2] = part(6)


def second_kernel(kept, fwd, bwd, far_fwd, far_bwd, out_fwd, out_bwd, own):
    half = far_fwd.shape[0]
    ahead = kept[1] + fwd[1].astype(F32)
    out_fwd[:half] = (ahead[:half] + far_fwd[...].astype(F32)).astype(BF16)
    out_fwd[half:] = ahead[half:].astype(BF16)
    behind = kept[2] + bwd[1].astype(F32)
    out_bwd[:half] = behind[:half].astype(BF16)
    out_bwd[half:] = (behind[half:] + far_bwd[...].astype(F32)).astype(BF16)
    own[...] = kept[0] + fwd[0].astype(F32) + bwd[0].astype(F32)


def last_kernel(own, fwd, bwd, rhs, inverse, solved):
    coupled = own[...] + (fwd[...].astype(F32) + bwd[...].astype(F32))
    residual = (rhs[...].astype(F32) - coupled).astype(BF16)
    solved[...] = jnp.dot(inverse[...], residual, preferred_element_type=F32).astype(BF16)


def call(kernel, outs, *args):
    return pl.pallas_call(
        kernel,
        out_shape=outs,
        in_specs=[whole()] * len(args),
        out_specs=[whole()] * len(outs),
        compiler_params=params(),
    )(*args)


def gather(part, first, second):
    fwd = move(part, first, 1)
    bwd = move(part, first, -1)
    far = move(part, first, 2)
    line = jnp.concatenate([part, bwd, far, fwd], 0)
    from_fwd = move(line, second, 1)
    from_bwd = move(line, second, -1)
    on_fwd = move(from_fwd[:2], second, 1)
    on_bwd = move(from_bwd[2:], second, -1)
    pieces = [line, from_bwd, on_fwd, on_bwd, from_fwd]
    places = [(0, 4), (4, 4), (8, 2), (10, 2), (12, 4)]
    return pieces, places


def local(rhs_one, inv_one, rhs_two, inv_two, blocks, block_rows, block_cols):
    rows = rhs_one.shape[3]
    row = lax.axis_index("row")
    col = lax.axis_index("col")
    core = col % 2
    sign = 1 - 2 * core
    here_y, here_x, here_z = row // 4, row % 4, col // 2

    target = block_rows[0, 0]
    parity = target % 2
    steps = ((1 - 2 * parity) * (target // 2 - here_z)) % 8
    target_slot = jnp.where(parity == core, 0, 8) + steps
    source = block_cols[0, 0]
    place = source // 2
    from_y = (sign * (place // 4 - here_y)) % 4
    from_x = (sign * (place % 4 - here_x)) % 4
    source_slot = jnp.where(source % 2 == 0, from_y * 4 + from_x, 16 + from_x * 4 + from_y)

    solved_one, *parts = solve_one(rhs_one[0, 0], inv_one[0, 0], WIDTHS)
    columns = []
    start = 0
    for i, width in enumerate(WIDTHS):
        pieces, places = gather(parts[2 * i], "x", "y")
        more, more_places = gather(parts[2 * i + 1], "y", "x")
        places = places + [(16 + s, n) for s, n in more_places]
        keep, send = couple(source_slot, target_slot, blocks[0, 0], pieces + more, places)
        other = swap_cores(send)
        half = shape((rows // 2, width))
        near = shape((2, rows, width))
        near_fwd, near_bwd, far_fwd, far_bwd, kept = call(
            first_kernel, [near, near, half, half, shape((3, rows, width), F32)], keep, other
        )
        near_fwd = move(near_fwd, "z", 1)
        near_bwd = move(near_bwd, "z", -1)
        far_fwd = move(far_fwd, "z", 2)
        far_bwd = move(far_bwd, "z", -2)
        one = shape((rows, width))
        out_fwd, out_bwd, own = call(
            second_kernel, [one, one, shape((rows, width), F32)], kept, near_fwd, near_bwd, far_fwd, far_bwd
        )
        out_fwd = move(out_fwd, "z", 2)
        out_bwd = move(out_bwd, "z", -2)
        (column,) = call(
            last_kernel, [one], own, out_fwd, out_bwd, rhs_two[0, 0, 0, :, start : start + width], inv_two[0, 0, 0]
        )
        columns.append(column)
        start += width
    solved_two = columns[0] if len(columns) == 1 else jnp.concatenate(columns, 1)
    return (solved_one[None, None], solved_two[None, None, None])


def solution(mesh):
    in_specs = (
        P("row", "col", None, None, None),
        P("row", "col", None, None, None),
        P("row", "col", None, None, None),
        P("row", "col", None, None, None),
        P("row", "col", None, None, None),
        P("row", "col", None),
        P("row", "col", None),
    )
    out_specs = (P("row", "col", None, None, None), P("row", "col", None, None, None))
    return jax.shard_map(local, mesh=mesh, in_specs=in_specs, out_specs=out_specs, check_vma=False)
```

```python
import functools

import jax
import jax.numpy as jnp
from jax import lax
from jax.experimental import pallas as pl
from jax.experimental.pallas import tpu as pltpu
from jax.sharding import PartitionSpec as P

PARTS = 1
STEP = 8
BOTH = ("row", "col")
MIB = 1024 * 1024
F32 = jnp.float32
BF16 = jnp.bfloat16


def whole(memory=pltpu.VMEM):
    return pl.BlockSpec(memory_space=memory)


def shape(dims, dtype=BF16):
    return jax.ShapeDtypeStruct(dims, dtype)


def params(mib=16):
    return pltpu.CompilerParams(vmem_limit_bytes=mib * MIB)


def ring_pairs(axis, steps):
    pairs = []
    for y in range(4):
        for x in range(4):
            for z in range(8):
                for core in range(2):
                    way = steps if core == 0 else -steps
                    to_y, to_x, to_z = y, x, z
                    if axis == "x":
                        to_x = (x + way) % 4
                    elif axis == "y":
                        to_y = (y + way) % 4
                    else:
                        to_z = (z + way) % 8
                    pairs.append(((y * 4 + x) * 16 + z * 2 + core, (to_y * 4 + to_x) * 16 + to_z * 2 + core))
    return pairs


def move(value, axis, steps):
    return lax.ppermute(value, BOTH, ring_pairs(axis, steps))


def swap_cores(value):
    return lax.ppermute(value, "col", [(i, i ^ 1) for i in range(16)])


def solve_one_kernel(rhs_hbm, inverse_hbm, solved, even, odd, rhs, inverse, sems):
    copies = []
    for q in range(2):
        copies.append(pltpu.make_async_copy(rhs_hbm.at[q], rhs.at[q], sems.at[2 * q]))
        copies.append(pltpu.make_async_copy(inverse_hbm.at[q], inverse.at[q], sems.at[2 * q + 1]))
    for copy in copies:
        copy.start()
    for q, out in enumerate((even, odd)):
        copies[2 * q].wait()
        copies[2 * q + 1].wait()
        value = jnp.dot(inverse[q], rhs[q], preferred_element_type=F32).astype(BF16)
        solved[q] = value
        width = value.shape[1] // PARTS
        for i in range(PARTS):
            out[i] = value[:, i * width : (i + 1) * width]


def solve_one(rhs, inverse):
    part = shape((PARTS, rhs.shape[1], rhs.shape[2] // PARTS))
    return pl.pallas_call(
        solve_one_kernel,
        out_shape=[shape(rhs.shape), part, part],
        in_specs=[whole(pltpu.HBM)] * 2,
        out_specs=[whole()] * 3,
        scratch_shapes=[
            pltpu.VMEM(rhs.shape, BF16),
            pltpu.VMEM(inverse.shape, BF16),
            pltpu.SemaphoreType.DMA((4,)),
        ],
        compiler_params=params(),
    )(*[pltpu.with_memory_space_constraint(value, pltpu.HBM) for value in (rhs, inverse)])


def stage_kernel(blocks_hbm, blocks, sems):
    size = blocks.shape[0] // STEP
    copies = []
    for i in range(size):
        span = pl.ds(i * STEP, STEP)
        copies.append(pltpu.make_async_copy(blocks_hbm.at[span], blocks.at[span], sems.at[i]))
        copies[-1].start()
    for copy in copies:
        copy.wait()


def stage(blocks):
    return pl.pallas_call(
        stage_kernel,
        out_shape=pltpu.VMEM(blocks.shape, blocks.dtype),
        in_specs=[whole(pl.ANY)],
        out_specs=whole(),
        scratch_shapes=[pltpu.SemaphoreType.DMA((blocks.shape[0] // STEP,))],
        compiler_params=params(4),
    )(pltpu.with_memory_space_constraint(blocks, pltpu.HBM))


def couple_kernel(slots, count, chosen, source_slot, target_slot, blocks, *refs):
    pieces = refs[:slots]
    total, send, sources, sems = refs[slots:]
    copies = []
    for i, piece in enumerate(pieces):
        copies.append(pltpu.make_async_copy(piece, sources.at[pl.ds(4 * i, 4)], sems.at[i]))
        copies[-1].start()
    total[...] = jnp.zeros_like(total)
    for copy in copies:
        copy.wait()

    def products(group, carry):
        for j in range(STEP):
            index = group * STEP + j
            product = jnp.dot(blocks[chosen[index]], sources[source_slot[index]], preferred_element_type=F32)
            total[target_slot[index]] += product
        return carry

    lax.fori_loop(0, (count[0] + STEP - 1) // STEP, products, 0)
    send[...] = total[8:16].astype(BF16)


def couple(picked, blocks, pieces):
    count, rows, _ = blocks.shape
    width = pieces[0].shape[-1]
    return pl.pallas_call(
        functools.partial(couple_kernel, len(pieces)),
        out_shape=[pltpu.VMEM((17, rows, width), F32), shape((8, rows, width))],
        in_specs=[whole(pltpu.SMEM)] * 4 + [whole()] + [whole(pl.ANY)] * len(pieces),
        out_specs=[whole()] * 2,
        scratch_shapes=[
            pltpu.VMEM((4 * len(pieces), rows, width), BF16),
            pltpu.SemaphoreType.DMA((len(pieces),)),
        ],
        compiler_params=params(16),
        cost_estimate=pl.CostEstimate(
            flops=2 * count * rows * rows * width, bytes_accessed=2 * count * rows * rows, transcendentals=0
        ),
    )(*picked, pltpu.with_memory_space_constraint(blocks, pltpu.VMEM), *pieces)


def pick(wanted, source_slot, target_slot):
    size = wanted.shape[0]
    index = jnp.arange(size, dtype=jnp.int32)
    place = jnp.cumsum(wanted.astype(jnp.int32)) - 1
    hits = wanted[None, :] & (place[None, :] == index[:, None])
    gathered = lambda values: jnp.sum(jnp.where(hits, values[None, :], 0), axis=1, dtype=jnp.int32)
    found = jnp.sum(wanted, dtype=jnp.int32)
    target = jnp.where(index < found, gathered(target_slot), 16)
    return found.reshape(1), gathered(index), gathered(source_slot), target


ORDER = (1, 3, 7, 5, 4, 2, 6, 0)
PLACES = tuple(ORDER.index(u) for u in range(8))


def merge_kernel(keep, other, base):
    base[...] = keep[:8] + other[...].astype(F32)


def first_kernel(bases, keep, other, *refs):
    base = refs[:bases]
    fwd, bwd, far, held = refs[bases:]

    def part(place):
        value = keep[place] + other[place].astype(F32)
        return value + base[0][place] if bases else value

    fwd[0] = part(0).astype(BF16)
    fwd[1] = part(1).astype(BF16)
    bwd[0] = part(2).astype(BF16)
    bwd[1] = part(3).astype(BF16)
    far[...] = part(4).astype(BF16)
    for i in range(3):
        held[i] = part(5 + i)


def second_kernel(held, fwd, bwd, far, out_fwd, out_bwd, own):
    out_fwd[...] = (held[0] + (fwd[1].astype(F32) + far[...].astype(F32))).astype(BF16)
    out_bwd[...] = (held[1] + bwd[1].astype(F32)).astype(BF16)
    own[...] = held[2] + (fwd[0].astype(F32) + bwd[0].astype(F32))


def last_kernel(own, fwd, bwd, rhs, inverse, solved):
    coupled = own[...] + (fwd[...].astype(F32) + bwd[...].astype(F32))
    residual = (rhs[...].astype(F32) - coupled).astype(BF16)
    solved[...] = jnp.dot(inverse[...], residual, preferred_element_type=F32).astype(BF16)


def call(kernel, outs, *args):
    return pl.pallas_call(
        kernel,
        out_shape=outs,
        in_specs=[whole()] * len(args),
        out_specs=[whole()] * len(outs),
        compiler_params=params(),
    )(*args)


def after(value, *others):
    return lax.optimization_barrier((value, *others))[0]


def line_of(part, axis):
    fwd = move(part, axis, 1)
    bwd = move(part, axis, -1)
    far = move(part, axis, 2)
    return [jnp.stack([part[i], bwd[i], far[i], fwd[i]]) for i in range(PARTS)]


def reduce_along_z(base, keep, other):
    _, rows, width = other.shape
    one = shape((rows, width))
    two = shape((2, rows, width))
    kernel = functools.partial(first_kernel, len(base))
    fwd, bwd, far, held = call(kernel, [two, two, one, shape((3, rows, width), F32)], keep, other, *base)
    fwd = move(fwd, "z", 1)
    bwd = move(bwd, "z", -1)
    far = move(far, "z", 2)
    sent = (fwd, bwd, far)
    out_fwd, out_bwd, own = call(second_kernel, [one, one, shape((rows, width), F32)], held, fwd, bwd, far)
    out_fwd = move(out_fwd, "z", 2)
    out_bwd = move(out_bwd, "z", -2)
    return (own, out_fwd, out_bwd), sent


def local(rhs_one, inv_one, rhs_two, inv_two, blocks, block_rows, block_cols):
    rows = rhs_one.shape[3]
    row = lax.axis_index("row")
    col = lax.axis_index("col")
    core = col % 2
    sign = 1 - 2 * core
    here_y, here_x, here_z = row // 4, row % 4, col // 2

    target = block_rows[0, 0]
    parity = target % 2
    steps = ((1 - 2 * parity) * (target // 2 - here_z)) % 8
    target_slot = jnp.where(parity == core, 0, 8) + jnp.array(PLACES, jnp.int32)[steps]
    source = block_cols[0, 0]
    place = source // 2
    from_y = (sign * (place // 4 - here_y)) % 4
    from_x = (sign * (place % 4 - here_x)) % 4
    even = source % 2 == 0
    near = jnp.where(even, from_x, from_y)
    distant = jnp.where(even, from_y, from_x)
    later = distant == 2
    early_slot = jnp.where(even, 0, 12) + jnp.where(distant == 3, 2, distant) * 4 + near
    early_picked = pick(jnp.logical_not(later), early_slot, target_slot)
    later_picked = pick(later, jnp.where(even, 0, 4) + near, target_slot)
    all_slot = jnp.where(later, jnp.where(even, 24, 28) + near, early_slot)
    all_picked = (jnp.full((1,), target.shape[0], jnp.int32), jnp.arange(target.shape[0], dtype=jnp.int32), all_slot, target_slot)

    solved_one, even, odd = solve_one(rhs_one[0, 0], inv_one[0, 0])
    lines = list(zip(line_of(even, "x"), line_of(odd, "y")))
    factor = stage(blocks[0, 0])
    axes = ("y", "x")
    both = range(2)
    sums = []

    if PARTS == 2:
        line = lines[0]
        fwd = [move(line[q], axes[q], 1) for q in both]
        bwd = [move(line[q], axes[q], -1) for q in both]
        far = [move(fwd[q], axes[q], 1) for q in both]
        line = lines[1]
        next_fwd = [move(after(line[q], *bwd), axes[q], 1) for q in both]
        next_bwd = [move(after(line[q], *bwd), axes[q], -1) for q in both]
        pieces = [lines[0][0], bwd[0], fwd[0], lines[0][1], bwd[1], fwd[1], far[0], far[1]]
        keep, send = couple(all_picked, factor, pieces)
        far = [move(after(next_fwd[q], send), axes[q], 1) for q in both]
        fwd, bwd = next_fwd, next_bwd
        done, sent = reduce_along_z([], keep, swap_cores(send))
        sums.append(done)
    else:
        line = lines[0]
        fwd = [move(line[q], axes[q], 1) for q in both]
        bwd = [move(line[q], axes[q], -1) for q in both]
        far = [move(fwd[q], axes[q], 1) for q in both]
        sent = ()

    pieces = [line[0], bwd[0], fwd[0], line[1], bwd[1], fwd[1]]
    keep, send = couple(early_picked, factor, pieces)
    (base,) = call(merge_kernel, [shape(send.shape, F32)], keep, swap_cores(send))
    keep, send = couple(later_picked, factor, [after(far[0], *sent), far[1]])
    done, _ = reduce_along_z([base], keep, swap_cores(send))
    sums.append(done)

    width = rhs_two.shape[4] // PARTS
    columns = []
    for i, done in enumerate(sums):
        rhs = rhs_two[0, 0, 0, :, i * width : (i + 1) * width]
        columns += call(last_kernel, [shape((rows, width))], *done, rhs, inv_two[0, 0, 0])
    solved_two = jnp.concatenate(columns, 1)
    return (solved_one[None, None], solved_two[None, None, None])


def solution(mesh):
    in_specs = (
        P("row", "col", None, None, None),
        P("row", "col", None, None, None),
        P("row", "col", None, None, None),
        P("row", "col", None, None, None),
        P("row", "col", None, None, None),
        P("row", "col", None),
        P("row", "col", None),
    )
    out_specs = (P("row", "col", None, None, None), P("row", "col", None, None, None))
    return jax.shard_map(local, mesh=mesh, in_specs=in_specs, out_specs=out_specs, check_vma=False)
```

```python
import functools

import jax
import jax.numpy as jnp
from jax import lax
from jax.experimental import pallas as pl
from jax.experimental.pallas import tpu as pltpu
from jax.sharding import PartitionSpec as P

PARTS = 2
STEP = 16
BOTH = ("row", "col")
MIB = 1024 * 1024
F32 = jnp.float32
BF16 = jnp.bfloat16


def whole(memory=pltpu.VMEM):
    return pl.BlockSpec(memory_space=memory)


def shape(dims, dtype=BF16):
    return jax.ShapeDtypeStruct(dims, dtype)


def params(mib=16):
    return pltpu.CompilerParams(vmem_limit_bytes=mib * MIB)


def ring_pairs(axis, steps):
    pairs = []
    for y in range(4):
        for x in range(4):
            for z in range(8):
                for core in range(2):
                    way = steps if core == 0 else -steps
                    to_y, to_x, to_z = y, x, z
                    if axis == "x":
                        to_x = (x + way) % 4
                    elif axis == "y":
                        to_y = (y + way) % 4
                    else:
                        to_z = (z + way) % 8
                    pairs.append(((y * 4 + x) * 16 + z * 2 + core, (to_y * 4 + to_x) * 16 + to_z * 2 + core))
    return pairs


def move(value, axis, steps):
    return lax.ppermute(value, BOTH, ring_pairs(axis, steps))


def swap_cores(value):
    return lax.ppermute(value, "col", [(i, i ^ 1) for i in range(16)])


def solve_one_kernel(rhs_hbm, inverse_hbm, solved, even, odd, rhs, inverse, sems):
    copies = []
    for q in range(2):
        copies.append(pltpu.make_async_copy(rhs_hbm.at[q], rhs.at[q], sems.at[2 * q]))
        copies.append(pltpu.make_async_copy(inverse_hbm.at[q], inverse.at[q], sems.at[2 * q + 1]))
    for copy in copies:
        copy.start()
    for q, out in enumerate((even, odd)):
        copies[2 * q].wait()
        copies[2 * q + 1].wait()
        value = jnp.dot(inverse[q], rhs[q], preferred_element_type=F32).astype(BF16)
        solved[q] = value
        out[0] = value


def solve_one(rhs, inverse):
    part = shape((1, *rhs.shape[1:]))
    return pl.pallas_call(
        solve_one_kernel,
        out_shape=[shape(rhs.shape), part, part],
        in_specs=[whole(pltpu.HBM)] * 2,
        out_specs=[whole()] * 3,
        scratch_shapes=[
            pltpu.VMEM(rhs.shape, BF16),
            pltpu.VMEM(inverse.shape, BF16),
            pltpu.SemaphoreType.DMA((4,)),
        ],
        compiler_params=params(),
    )(*[pltpu.with_memory_space_constraint(value, pltpu.HBM) for value in (rhs, inverse)])


def stage_kernel(blocks_hbm, first_line, second_line, blocks, token, sems):
    size = blocks.shape[0] // STEP
    copies = []
    for i in range(size):
        span = pl.ds(i * STEP, STEP)
        copies.append(pltpu.make_async_copy(blocks_hbm.at[span], blocks.at[span], sems.at[i]))
        copies[-1].start()
    token[...] = jnp.zeros_like(token)
    for copy in copies:
        copy.wait()


def stage(blocks, lines):
    return pl.pallas_call(
        stage_kernel,
        out_shape=[pltpu.VMEM(blocks.shape, blocks.dtype), shape((8, 128), F32)],
        in_specs=[whole(pl.ANY)] * 3,
        out_specs=[whole()] * 2,
        scratch_shapes=[pltpu.SemaphoreType.DMA((blocks.shape[0] // STEP,))],
        compiler_params=params(4),
    )(pltpu.with_memory_space_constraint(blocks, pltpu.HBM), *lines)


def couple_kernel(size, start, count, chosen, source_slot, target_slot, blocks, *refs):
    pieces = refs[:size]
    total, send, sources, sems = refs[size:]
    width = sources.shape[2]
    copies = []
    for i, piece in enumerate(pieces):
        spot = sources.at[pl.ds(4 * i, 4)]
        copies.append(pltpu.make_async_copy(piece.at[:, :, pl.ds(start, width)], spot, sems.at[i]))
        copies[-1].start()
    total[...] = jnp.zeros_like(total)
    for copy in copies:
        copy.wait()

    def products(group, carry):
        for j in range(STEP):
            index = group * STEP + j
            product = jnp.dot(blocks[chosen[index]], sources[source_slot[index]], preferred_element_type=F32)
            total[target_slot[index]] += product
        return carry

    lax.fori_loop(0, (count[0] + STEP - 1) // STEP, products, 0)
    send[...] = total[8:16].astype(BF16)


def couple(picked, blocks, pieces, start, width):
    count, rows, _ = blocks.shape
    slots = 4 * len(pieces)
    return pl.pallas_call(
        functools.partial(couple_kernel, len(pieces), start),
        out_shape=[pltpu.VMEM((17, rows, width), F32), shape((8, rows, width))],
        in_specs=[whole(pltpu.SMEM)] * 4 + [whole()] + [whole(pl.ANY)] * len(pieces),
        out_specs=[whole()] * 2,
        scratch_shapes=[
            pltpu.VMEM((slots, rows, width), BF16),
            pltpu.SemaphoreType.DMA((len(pieces),)),
        ],
        compiler_params=params(16),
        cost_estimate=pl.CostEstimate(
            flops=2 * count * rows * rows * width, bytes_accessed=2 * count * rows * rows, transcendentals=0
        ),
    )(*picked, pltpu.with_memory_space_constraint(blocks, pltpu.VMEM), *pieces)


def pick(wanted, source_slot, target_slot):
    size = wanted.shape[0]
    index = jnp.arange(size, dtype=jnp.int32)
    place = jnp.cumsum(wanted.astype(jnp.int32)) - 1
    hits = wanted[None, :] & (place[None, :] == index[:, None])
    gathered = lambda values: jnp.sum(jnp.where(hits, values[None, :], 0), axis=1, dtype=jnp.int32)
    found = jnp.sum(wanted, dtype=jnp.int32)
    target = jnp.where(index < found, gathered(target_slot), 16)
    return found.reshape(1), gathered(index), gathered(source_slot), target


ORDER = (1, 3, 7, 5, 4, 2, 6, 0)
PLACES = tuple(ORDER.index(u) for u in range(8))


def merge_kernel(keep, other, base):
    base[...] = keep[:8] + other[...].astype(F32)


def first_kernel(column, base, keep, other, fwd, bwd, far, held):
    def part(place):
        width = keep.shape[2]
        early = base[place, :, column : column + width]
        return early + (keep[place] + other[place].astype(F32))

    fwd[0] = part(0).astype(BF16)
    fwd[1] = part(1).astype(BF16)
    bwd[0] = part(2).astype(BF16)
    bwd[1] = part(3).astype(BF16)
    far[...] = part(4).astype(BF16)
    for i in range(3):
        held[i] = part(5 + i)


def second_kernel(held, fwd, bwd, far, out_fwd, out_bwd, own):
    out_fwd[...] = (held[0] + (fwd[1].astype(F32) + far[...].astype(F32))).astype(BF16)
    out_bwd[...] = (held[1] + bwd[1].astype(F32)).astype(BF16)
    own[...] = held[2] + (fwd[0].astype(F32) + bwd[0].astype(F32))


def last_kernel(start, own, fwd, bwd, rhs, inverse, *refs):
    solved = refs[-1]
    width = own.shape[1]
    coupled = own[...] + (fwd[...].astype(F32) + bwd[...].astype(F32))
    residual = (rhs[:, start : start + width].astype(F32) - coupled).astype(BF16)
    value = jnp.dot(inverse[...], residual, preferred_element_type=F32).astype(BF16)
    if start:
        solved[:, :start] = refs[0][...]
    solved[:, start : start + width] = value


def call(kernel, outs, *args):
    return pl.pallas_call(
        kernel,
        out_shape=outs,
        in_specs=[whole()] * len(args),
        out_specs=[whole()] * len(outs),
        compiler_params=params(),
    )(*args)


def after(value, *others):
    return lax.optimization_barrier((value, *others))[0]


def line_of(part, axis, direct):
    fwd = move(part, axis, 1)
    bwd = move(part, axis, -1)
    far = move(part, axis, 2) if direct else move(fwd, axis, 1)
    return jnp.concatenate([part, bwd, far, fwd])


def reduce_along_z(column, base, keep, other):
    _, rows, width = other.shape
    one = shape((rows, width))
    two = shape((2, rows, width))
    kernel = functools.partial(first_kernel, column)
    fwd, bwd, far, held = call(kernel, [two, two, one, shape((3, rows, width), F32)], base, keep, other)
    fwd = move(fwd, "z", 1)
    bwd = move(bwd, "z", -1)
    far = move(far, "z", 2)
    out_fwd, out_bwd, own = call(second_kernel, [one, one, shape((rows, width), F32)], held, fwd, bwd, far)
    out_fwd = move(out_fwd, "z", 2)
    out_bwd = move(out_bwd, "z", -2)
    return own, out_fwd, out_bwd


def local(rhs_one, inv_one, rhs_two, inv_two, blocks, block_rows, block_cols):
    rows = rhs_one.shape[3]
    row = lax.axis_index("row")
    col = lax.axis_index("col")
    core = col % 2
    sign = 1 - 2 * core
    here_y, here_x, here_z = row // 4, row % 4, col // 2

    target = block_rows[0, 0]
    parity = target % 2
    steps = ((1 - 2 * parity) * (target // 2 - here_z)) % 8
    target_slot = jnp.where(parity == core, 0, 8) + jnp.array(PLACES, jnp.int32)[steps]
    source = block_cols[0, 0]
    place = source // 2
    from_y = (sign * (place // 4 - here_y)) % 4
    from_x = (sign * (place % 4 - here_x)) % 4
    even = source % 2 == 0
    near = jnp.where(even, from_x, from_y)
    distant = jnp.where(even, from_y, from_x)
    ranks = jnp.where((distant == 1) | (distant == 2), 1, 0)
    slot = (jnp.where(even, 0, 2) + jnp.where((distant == 2) | (distant == 3), 1, 0)) * 4 + near
    early_picked = pick(ranks == 0, slot, target_slot)
    later_picked = pick(ranks == 1, slot, target_slot)

    solved_one, even, odd = solve_one(rhs_one[0, 0], inv_one[0, 0])
    lines = [line_of(even, "x", False), line_of(odd, "y", False)]
    axes = ("y", "x")
    both = range(2)

    fwd = [move(lines[q], axes[q], 1) for q in both]
    factor, token = stage(blocks[0, 0], lines)
    bwd = [move(after(lines[q], token), axes[q], -1) for q in both]
    far = [move(fwd[q], axes[q], 1) for q in both]

    whole_width = rhs_two.shape[4]
    pieces = [lines[0], fwd[0], lines[1], fwd[1]]
    keep, send = couple(early_picked, factor, pieces, 0, whole_width)
    (base,) = call(merge_kernel, [shape(send.shape, F32)], keep, swap_cores(send))
    width = whole_width // PARTS
    solved_two = []
    for i in range(PARTS):
        start = i * width
        keep, send = couple(later_picked, factor, [bwd[0], far[0], bwd[1], far[1]], start, width)
        sums = reduce_along_z(start, base, keep, swap_cores(send))
        kernel = functools.partial(last_kernel, start)
        solved_two = call(kernel, [shape((rows, start + width))], *sums, rhs_two[0, 0, 0], inv_two[0, 0, 0], *solved_two)
    return (solved_one[None, None], solved_two[0][None, None, None])


def solution(mesh):
    in_specs = (
        P("row", "col", None, None, None),
        P("row", "col", None, None, None),
        P("row", "col", None, None, None),
        P("row", "col", None, None, None),
        P("row", "col", None, None, None),
        P("row", "col", None),
        P("row", "col", None),
    )
    out_specs = (P("row", "col", None, None, None), P("row", "col", None, None, None))
    return jax.shard_map(local, mesh=mesh, in_specs=in_specs, out_specs=out_specs, check_vma=False)
```

```python
import functools

import jax
import jax.numpy as jnp
from jax import lax
from jax.experimental import pallas as pl
from jax.experimental.pallas import tpu as pltpu
from jax.sharding import PartitionSpec as P

PARTS = 2
STEP = 16
BOTH = ("row", "col")
MIB = 1024 * 1024
F32 = jnp.float32
BF16 = jnp.bfloat16


def whole(memory=pltpu.VMEM):
    return pl.BlockSpec(memory_space=memory)


def shape(dims, dtype=BF16):
    return jax.ShapeDtypeStruct(dims, dtype)


def params(mib=16):
    return pltpu.CompilerParams(vmem_limit_bytes=mib * MIB)


def ring_pairs(axis, steps):
    pairs = []
    for y in range(4):
        for x in range(4):
            for z in range(8):
                for core in range(2):
                    way = steps if core == 0 else -steps
                    to_y, to_x, to_z = y, x, z
                    if axis == "x":
                        to_x = (x + way) % 4
                    elif axis == "y":
                        to_y = (y + way) % 4
                    else:
                        to_z = (z + way) % 8
                    pairs.append(((y * 4 + x) * 16 + z * 2 + core, (to_y * 4 + to_x) * 16 + to_z * 2 + core))
    return pairs


def move(value, axis, steps):
    return lax.ppermute(value, BOTH, ring_pairs(axis, steps))


def swap_cores(value):
    return lax.ppermute(value, "col", [(i, i ^ 1) for i in range(16)])


def solve_one_kernel(rhs_hbm, inverse_hbm, solved, rhs, inverse, sems):
    copies = []
    for q in range(2):
        copies.append(pltpu.make_async_copy(rhs_hbm.at[q], rhs.at[q], sems.at[2 * q]))
        copies.append(pltpu.make_async_copy(inverse_hbm.at[q], inverse.at[q], sems.at[2 * q + 1]))
    for copy in copies:
        copy.start()
    for q in range(2):
        copies[2 * q].wait()
        copies[2 * q + 1].wait()
        solved[q] = jnp.dot(inverse[q], rhs[q], preferred_element_type=F32).astype(BF16)


def solve_one(rhs, inverse):
    return pl.pallas_call(
        solve_one_kernel,
        out_shape=shape(rhs.shape),
        in_specs=[whole(pltpu.HBM)] * 2,
        out_specs=whole(),
        scratch_shapes=[
            pltpu.VMEM(rhs.shape, BF16),
            pltpu.VMEM(inverse.shape, BF16),
            pltpu.SemaphoreType.DMA((4,)),
        ],
        compiler_params=params(),
    )(*[pltpu.with_memory_space_constraint(value, pltpu.HBM) for value in (rhs, inverse)])


def stage_kernel(blocks_hbm, first_line, second_line, blocks, first_same, second_same, sems):
    size = blocks.shape[0] // STEP
    copies = [
        pltpu.make_async_copy(first_line, first_same, sems.at[size]),
        pltpu.make_async_copy(second_line, second_same, sems.at[size + 1]),
    ]
    for i in range(size):
        span = pl.ds(i * STEP, STEP)
        copies.append(pltpu.make_async_copy(blocks_hbm.at[span], blocks.at[span], sems.at[i]))
    for copy in copies:
        copy.start()
    for copy in copies:
        copy.wait()


def stage(blocks, lines):
    return pl.pallas_call(
        stage_kernel,
        out_shape=[pltpu.VMEM(blocks.shape, blocks.dtype)] + [shape(line.shape) for line in lines],
        in_specs=[whole(pl.ANY)] * 3,
        out_specs=[whole()] + [whole(pl.ANY)] * 2,
        scratch_shapes=[pltpu.SemaphoreType.DMA((blocks.shape[0] // STEP + 2,))],
        compiler_params=params(4),
    )(pltpu.with_memory_space_constraint(blocks, pltpu.HBM), *lines)


def couple_kernel(size, start, goes_on, sends, count, chosen, source_slot, target_slot, blocks, *refs):
    pieces = refs[:size]
    refs = refs[size + goes_on :]
    total, sources, sems = refs[0], refs[-2], refs[-1]
    width = sources.shape[2]
    copies = []
    slot = 0
    for i, piece in enumerate(pieces):
        spot = sources.at[pl.ds(slot, piece.shape[0])]
        copies.append(pltpu.make_async_copy(piece.at[:, :, pl.ds(start, width)], spot, sems.at[i]))
        copies[-1].start()
        slot += piece.shape[0]
    if not goes_on:
        total[...] = jnp.zeros_like(total)
    for copy in copies:
        copy.wait()

    def products(group, carry):
        for j in range(STEP):
            index = group * STEP + j
            product = jnp.dot(blocks[chosen[index]], sources[source_slot[index]], preferred_element_type=F32)
            total[target_slot[index]] += product
        return carry

    lax.fori_loop(0, (count[0] + STEP - 1) // STEP, products, 0)
    if sends:
        refs[1][...] = total[8:16].astype(BF16)


def couple(picked, blocks, pieces, start, width, before=None, sends=True):
    count, rows, _ = blocks.shape
    goes_on = before is not None
    in_vmem = [pltpu.with_memory_space_constraint(value, pltpu.VMEM) for value in ([blocks, before] if goes_on else [blocks])]
    return pl.pallas_call(
        functools.partial(couple_kernel, len(pieces), start, int(goes_on), sends),
        out_shape=[pltpu.VMEM((17, rows, width), F32)] + [shape((8, rows, width))] * sends,
        in_specs=[whole(pltpu.SMEM)] * 4 + [whole()] + [whole(pl.ANY)] * len(pieces) + [whole()] * goes_on,
        out_specs=[whole()] * (1 + sends),
        scratch_shapes=[
            pltpu.VMEM((sum(piece.shape[0] for piece in pieces), rows, width), BF16),
            pltpu.SemaphoreType.DMA((len(pieces),)),
        ],
        input_output_aliases={5 + len(pieces): 0} if goes_on else {},
        compiler_params=params(16),
        cost_estimate=pl.CostEstimate(
            flops=2 * count * rows * rows * width, bytes_accessed=2 * count * rows * rows, transcendentals=0
        ),
    )(*picked, in_vmem[0], *pieces, *in_vmem[1:])


def pick(wanted, source_slot, target_slot):
    size = wanted.shape[0]
    index = jnp.arange(size, dtype=jnp.int32)
    place = jnp.cumsum(wanted.astype(jnp.int32)) - 1
    hits = wanted[None, :] & (place[None, :] == index[:, None])
    gathered = lambda values: jnp.sum(jnp.where(hits, values[None, :], 0), axis=1, dtype=jnp.int32)
    found = jnp.sum(wanted, dtype=jnp.int32)
    target = jnp.where(index < found, gathered(target_slot), 16)
    return found.reshape(1), gathered(index), gathered(source_slot), target


ORDER = (4, 2, 5, 3, 6, 1, 7, 0)
PLACES = tuple(ORDER.index(u) for u in range(8))


def first_kernel(column, early, early_other, keep, other, fwd, bwd, held):
    def part(place):
        columns = slice(column, column + keep.shape[2])
        known = early[place, :, columns] + early_other[place, :, columns].astype(F32)
        return known + (keep[place] + other[place].astype(F32))

    fwd[0] = part(0).astype(BF16)
    fwd[1] = part(1).astype(BF16)
    bwd[...] = part(2).astype(BF16)
    for i in range(5):
        held[i] = part(3 + i)


def second_kernel(held, fwd, bwd, out_fwd, out_bwd):
    out_fwd[...] = (held[0] + fwd[0].astype(F32)).astype(BF16)
    out_bwd[...] = (held[1] + bwd[...].astype(F32)).astype(BF16)


def third_kernel(held, near, fwd, bwd, out_fwd, out_bwd):
    out_fwd[...] = (held[2] + (near[1].astype(F32) + fwd[...].astype(F32))).astype(BF16)
    out_bwd[...] = (held[3] + bwd[...].astype(F32)).astype(BF16)


def last_kernel(start, held, fwd, bwd, rhs, inverse, *refs):
    solved = refs[-1]
    width = held.shape[2]
    coupled = held[4] + (fwd[...].astype(F32) + bwd[...].astype(F32))
    residual = (rhs[:, start : start + width].astype(F32) - coupled).astype(BF16)
    value = jnp.dot(inverse[...], residual, preferred_element_type=F32).astype(BF16)
    if start:
        solved[:, :start] = refs[0][...]
    solved[:, start : start + width] = value


def call(kernel, outs, *args):
    return pl.pallas_call(
        kernel,
        out_shape=outs,
        in_specs=[whole()] * len(args),
        out_specs=[whole()] * len(outs),
        compiler_params=params(),
    )(*args)


def reduce_along_z(column, early, early_other, keep, other):
    _, rows, width = other.shape
    one = shape((rows, width))
    kernel = functools.partial(first_kernel, column)
    outs = [shape((2, rows, width)), one, shape((5, rows, width), F32)]
    fwd, bwd, held = call(kernel, outs, early, early_other, keep, other)
    near = move(fwd, "z", 1)
    bwd = move(bwd, "z", -1)
    fwd, bwd = call(second_kernel, [one, one], held, near, bwd)
    fwd = move(fwd, "z", 2)
    bwd = move(bwd, "z", -1)
    fwd, bwd = call(third_kernel, [one, one], held, near, fwd, bwd)
    return held, move(fwd, "z", 1), move(bwd, "z", -1)


def again_kernel(value, same, sem):
    copy = pltpu.make_async_copy(value, same, sem)
    copy.start()
    copy.wait()


def again(value):
    return pl.pallas_call(
        again_kernel,
        out_shape=shape(value.shape),
        in_specs=[whole(pl.ANY)],
        out_specs=whole(pl.ANY),
        scratch_shapes=[pltpu.SemaphoreType.DMA],
        compiler_params=params(1),
    )(value)


def local(rhs_one, inv_one, rhs_two, inv_two, blocks, block_rows, block_cols):
    rows = rhs_one.shape[3]
    row = lax.axis_index("row")
    col = lax.axis_index("col")
    core = col % 2
    sign = 1 - 2 * core
    here_y, here_x, here_z = row // 4, row % 4, col // 2

    target = block_rows[0, 0]
    parity = target % 2
    steps = ((1 - 2 * parity) * (target // 2 - here_z)) % 8
    target_slot = jnp.where(parity == core, 0, 8) + jnp.array(PLACES, jnp.int32)[steps]
    source = block_cols[0, 0]
    place = source // 2
    from_y = (sign * (place // 4 - here_y)) % 4
    from_x = (sign * (place % 4 - here_x)) % 4
    q = source % 2
    near = jnp.where(q == 0, from_x, from_y)
    distant = jnp.where(q == 0, from_y, from_x)
    first_phase = (near == 0) | (distant == 0)
    across = 3 * q + near - 1
    first_slot = jnp.where(from_y == 0, 2 * from_x, jnp.where(from_x == 0, 6 + 2 * from_y, 0)) + q
    turn = jnp.where(first_phase | (distant == 3), 0, distant)
    picked = [
        pick(turn == 0, jnp.where(first_phase, first_slot, 14 + across), target_slot),
        pick(turn == 1, across, target_slot),
        pick(turn == 2, across, target_slot),
    ]

    solved_one = solve_one(rhs_one[0, 0], inv_one[0, 0])
    axes = ("x", "y")
    both = range(2)
    fwd = [move(solved_one, axis, 1) for axis in axes]
    solved_later = again(solved_one)
    bwd = [move(solved_later, axis, -1) for axis in axes]
    far = [move(fwd[i], axes[i], 1) for i in both]
    pieces = [solved_one] + [piece for i in both for piece in (bwd[i], far[i], fwd[i])]

    lines = [jnp.concatenate([bwd[q][q : q + 1], far[q][q : q + 1], fwd[q][q : q + 1]]) for q in both]
    fwd = [move(lines[q], axes[1 - q], 1) for q in both]
    factor, *lines = stage(blocks[0, 0], lines)
    bwd = [move(lines[q], axes[1 - q], -1) for q in both]
    far = [move(fwd[q], axes[1 - q], 1) for q in both]

    whole_width = rhs_two.shape[4]
    (early,) = couple(picked[0], factor, pieces + fwd, 0, whole_width, sends=False)
    early, send = couple(picked[1], factor, bwd, 0, whole_width, before=early)
    early_other = swap_cores(send)
    width = whole_width // PARTS
    solved_two = []
    for i in range(PARTS):
        start = i * width
        keep, send = couple(picked[2], factor, far, start, width)
        held, fwd, bwd = reduce_along_z(start, early, early_other, keep, swap_cores(send))
        kernel = functools.partial(last_kernel, start)
        solved_two = call(
            kernel, [shape((rows, start + width))], held, fwd, bwd, rhs_two[0, 0, 0], inv_two[0, 0, 0], *solved_two
        )
    return (solved_one[None, None], solved_two[0][None, None, None])


def solution(mesh):
    in_specs = (
        P("row", "col", None, None, None),
        P("row", "col", None, None, None),
        P("row", "col", None, None, None),
        P("row", "col", None, None, None),
        P("row", "col", None, None, None),
        P("row", "col", None),
        P("row", "col", None),
    )
    out_specs = (P("row", "col", None, None, None), P("row", "col", None, None, None))
    return jax.shard_map(local, mesh=mesh, in_specs=in_specs, out_specs=out_specs, check_vma=False)
```

```python
import functools

import jax
import jax.numpy as jnp
from jax import lax
from jax.experimental import pallas as pl
from jax.experimental.pallas import tpu as pltpu
from jax.sharding import PartitionSpec as P

PARTS = 2
STEP = 16
BOTH = ("row", "col")
MIB = 1024 * 1024
F32 = jnp.float32
BF16 = jnp.bfloat16


def whole(memory=pltpu.VMEM):
    return pl.BlockSpec(memory_space=memory)


def shape(dims, dtype=BF16):
    return jax.ShapeDtypeStruct(dims, dtype)


def params(mib=16):
    return pltpu.CompilerParams(vmem_limit_bytes=mib * MIB)


def ring_pairs(axis, steps):
    pairs = []
    for y in range(4):
        for x in range(4):
            for z in range(8):
                for core in range(2):
                    way = steps if core == 0 else -steps
                    to_y, to_x, to_z = y, x, z
                    if axis == "x":
                        to_x = (x + way) % 4
                    elif axis == "y":
                        to_y = (y + way) % 4
                    else:
                        to_z = (z + way) % 8
                    pairs.append(((y * 4 + x) * 16 + z * 2 + core, (to_y * 4 + to_x) * 16 + to_z * 2 + core))
    return pairs


def move(value, axis, steps):
    return lax.ppermute(value, BOTH, ring_pairs(axis, steps))


def swap_cores(value):
    return lax.ppermute(value, "col", [(i, i ^ 1) for i in range(16)])


def solve_one_kernel(rhs_hbm, inverse_hbm, solved, rhs, inverse, sems):
    copies = []
    for q in range(2):
        copies.append(pltpu.make_async_copy(rhs_hbm.at[q], rhs.at[q], sems.at[2 * q]))
        copies.append(pltpu.make_async_copy(inverse_hbm.at[q], inverse.at[q], sems.at[2 * q + 1]))
    for copy in copies:
        copy.start()
    for q in range(2):
        copies[2 * q].wait()
        copies[2 * q + 1].wait()
        solved[q] = jnp.dot(inverse[q], rhs[q], preferred_element_type=F32).astype(BF16)


def solve_one(rhs, inverse):
    return pl.pallas_call(
        solve_one_kernel,
        out_shape=shape(rhs.shape),
        in_specs=[whole(pltpu.HBM)] * 2,
        out_specs=whole(),
        scratch_shapes=[
            pltpu.VMEM(rhs.shape, BF16),
            pltpu.VMEM(inverse.shape, BF16),
            pltpu.SemaphoreType.DMA((4,)),
        ],
        compiler_params=params(),
    )(*[pltpu.with_memory_space_constraint(value, pltpu.HBM) for value in (rhs, inverse)])


def stage_kernel(blocks_hbm, first_line, second_line, blocks, first_same, second_same, sems):
    size = blocks.shape[0] // STEP
    copies = [
        pltpu.make_async_copy(first_line, first_same, sems.at[size]),
        pltpu.make_async_copy(second_line, second_same, sems.at[size + 1]),
    ]
    for i in range(size):
        span = pl.ds(i * STEP, STEP)
        copies.append(pltpu.make_async_copy(blocks_hbm.at[span], blocks.at[span], sems.at[i]))
    for copy in copies:
        copy.start()
    for copy in copies:
        copy.wait()


def stage(blocks, lines):
    return pl.pallas_call(
        stage_kernel,
        out_shape=[pltpu.VMEM(blocks.shape, blocks.dtype)] + [shape(line.shape) for line in lines],
        in_specs=[whole(pl.ANY)] * 3,
        out_specs=[whole()] + [whole(pl.ANY)] * 2,
        scratch_shapes=[pltpu.SemaphoreType.DMA((blocks.shape[0] // STEP + 2,))],
        compiler_params=params(4),
    )(pltpu.with_memory_space_constraint(blocks, pltpu.HBM), *lines)


def couple_kernel(turn, size, start, goes_on, sends, picked, blocks, *refs):
    pieces = refs[:size]
    refs = refs[size + goes_on :]
    total, sources, sems = refs[0], refs[-2], refs[-1]
    width = sources.shape[2]
    copies = []
    slot = 0
    for i, piece in enumerate(pieces):
        spot = sources.at[pl.ds(slot, piece.shape[0])]
        copies.append(pltpu.make_async_copy(piece.at[:, :, pl.ds(start, width)], spot, sems.at[i]))
        copies[-1].start()
        slot += piece.shape[0]
    if not goes_on:
        total[...] = jnp.zeros_like(total)
    for copy in copies:
        copy.wait()

    def products(group, carry):
        for j in range(STEP):
            entry = picked[turn, group * STEP + j]
            block, source, target = entry >> 11, (entry >> 5) & 63, 16 - (entry & 31)
            total[target] += jnp.dot(blocks[block], sources[source], preferred_element_type=F32)
        return carry

    def more(group):
        return (group < blocks.shape[0] // STEP) & (picked[turn, jnp.minimum(group * STEP, blocks.shape[0] - 1)] != 0)

    lax.while_loop(more, lambda group: products(group, group + 1), 0)
    if sends:
        refs[1][...] = total[8:16].astype(BF16)


def couple(turn, picked, blocks, pieces, start, width, before=None, sends=True):
    count, rows, _ = blocks.shape
    goes_on = before is not None
    in_vmem = [pltpu.with_memory_space_constraint(value, pltpu.VMEM) for value in ([blocks, before] if goes_on else [blocks])]
    return pl.pallas_call(
        functools.partial(couple_kernel, turn, len(pieces), start, int(goes_on), sends),
        out_shape=[pltpu.VMEM((17, rows, width), F32)] + [shape((8, rows, width))] * sends,
        in_specs=[whole(pltpu.SMEM)] + [whole()] + [whole(pl.ANY)] * len(pieces) + [whole()] * goes_on,
        out_specs=[whole()] * (1 + sends),
        scratch_shapes=[
            pltpu.VMEM((sum(piece.shape[0] for piece in pieces), rows, width), BF16),
            pltpu.SemaphoreType.DMA((len(pieces),)),
        ],
        input_output_aliases={2 + len(pieces): 0} if goes_on else {},
        compiler_params=params(16),
        cost_estimate=pl.CostEstimate(
            flops=2 * count * rows * rows * width, bytes_accessed=2 * count * rows * rows, transcendentals=0
        ),
    )(picked, in_vmem[0], *pieces, *in_vmem[1:])


def pick(turn, turns, source_slot, target_slot):
    size = turn.shape[0]
    index = jnp.arange(size, dtype=jnp.int32)
    wanted = turn[None, :] == jnp.arange(turns, dtype=jnp.int32)[:, None]
    before = index[None, :] < index[:, None]
    place = jnp.sum(wanted[:, None, :] & before[None], axis=2, dtype=jnp.int32)
    hits = wanted[:, None, :] & (place[:, None, :] == index[None, :, None])
    packed = (index * 64 + source_slot) * 32 + (16 - target_slot)
    return jnp.sum(jnp.where(hits, packed[None, None, :], 0), axis=2, dtype=jnp.int32)


ORDER = (4, 2, 5, 3, 6, 1, 7, 0)
PLACES = tuple(ORDER.index(u) for u in range(8))


def first_kernel(column, early, early_other, keep, other, fwd, bwd, held):
    def part(place):
        columns = slice(column, column + keep.shape[2])
        known = early[place, :, columns] + early_other[place, :, columns].astype(F32)
        return known + (keep[place] + other[place].astype(F32))

    fwd[0] = part(0).astype(BF16)
    fwd[1] = part(1).astype(BF16)
    bwd[...] = part(2).astype(BF16)
    for i in range(5):
        held[i] = part(3 + i)


def second_kernel(held, fwd, bwd, out_fwd, out_bwd):
    out_fwd[...] = (held[0] + fwd[0].astype(F32)).astype(BF16)
    out_bwd[...] = (held[1] + bwd[...].astype(F32)).astype(BF16)


def third_kernel(held, near, fwd, bwd, out_fwd, out_bwd):
    out_fwd[...] = (held[2] + (near[1].astype(F32) + fwd[...].astype(F32))).astype(BF16)
    out_bwd[...] = (held[3] + bwd[...].astype(F32)).astype(BF16)


def last_kernel(start, held, fwd, bwd, rhs, inverse, *refs):
    solved = refs[-1]
    width = held.shape[2]
    coupled = held[4] + (fwd[...].astype(F32) + bwd[...].astype(F32))
    residual = (rhs[:, start : start + width].astype(F32) - coupled).astype(BF16)
    value = jnp.dot(inverse[...], residual, preferred_element_type=F32).astype(BF16)
    if start:
        solved[:, :start] = refs[0][...]
    solved[:, start : start + width] = value


def call(kernel, outs, *args):
    return pl.pallas_call(
        kernel,
        out_shape=outs,
        in_specs=[whole()] * len(args),
        out_specs=[whole()] * len(outs),
        compiler_params=params(),
    )(*args)


def reduce_along_z(column, early, early_other, keep, other):
    _, rows, width = other.shape
    one = shape((rows, width))
    kernel = functools.partial(first_kernel, column)
    outs = [shape((2, rows, width)), one, shape((5, rows, width), F32)]
    fwd, bwd, held = call(kernel, outs, early, early_other, keep, other)
    near = move(fwd, "z", 1)
    bwd = move(bwd, "z", -1)
    fwd, bwd = call(second_kernel, [one, one], held, near, bwd)
    fwd = move(fwd, "z", 2)
    bwd = move(bwd, "z", -1)
    fwd, bwd = call(third_kernel, [one, one], held, near, fwd, bwd)
    return held, move(fwd, "z", 1), move(bwd, "z", -1)


def again_kernel(value, same, sem):
    copy = pltpu.make_async_copy(value, same, sem)
    copy.start()
    copy.wait()


def again(value):
    return pl.pallas_call(
        again_kernel,
        out_shape=shape(value.shape),
        in_specs=[whole(pl.ANY)],
        out_specs=whole(pl.ANY),
        scratch_shapes=[pltpu.SemaphoreType.DMA],
        compiler_params=params(1),
    )(value)


def local(rhs_one, inv_one, rhs_two, inv_two, blocks, block_rows, block_cols):
    rows = rhs_one.shape[3]
    row = lax.axis_index("row")
    col = lax.axis_index("col")
    core = col % 2
    sign = 1 - 2 * core
    here_y, here_x, here_z = row // 4, row % 4, col // 2

    target = block_rows[0, 0]
    parity = target % 2
    steps = ((1 - 2 * parity) * (target // 2 - here_z)) % 8
    target_slot = jnp.where(parity == core, 0, 8) + jnp.array(PLACES, jnp.int32)[steps]
    source = block_cols[0, 0]
    place = source // 2
    from_y = (sign * (place // 4 - here_y)) % 4
    from_x = (sign * (place % 4 - here_x)) % 4
    q = source % 2
    near = jnp.where(q == 0, from_x, from_y)
    distant = jnp.where(q == 0, from_y, from_x)
    first_phase = (near == 0) | (distant == 0)
    across = 3 * q + near - 1
    first_slot = jnp.where(from_y == 0, 2 * from_x, jnp.where(from_x == 0, 6 + 2 * from_y, 0)) + q
    turn = jnp.where(first_phase | (distant == 3), 0, distant)
    picked = pick(turn, 3, jnp.where(first_phase, first_slot, jnp.where(turn == 0, 14, 0) + across), target_slot)

    solved_one = solve_one(rhs_one[0, 0], inv_one[0, 0])
    axes = ("x", "y")
    both = range(2)
    fwd = [move(solved_one, axis, 1) for axis in axes]
    solved_later = again(solved_one)
    bwd = [move(solved_later, axis, -1) for axis in axes]
    far = [move(fwd[i], axes[i], 1) for i in both]
    pieces = [solved_one] + [piece for i in both for piece in (bwd[i], far[i], fwd[i])]

    lines = [jnp.concatenate([bwd[q][q : q + 1], far[q][q : q + 1], fwd[q][q : q + 1]]) for q in both]
    fwd = [move(lines[q], axes[1 - q], 1) for q in both]
    factor, *lines = stage(blocks[0, 0], lines)
    bwd = [move(lines[q], axes[1 - q], -1) for q in both]
    far = [move(fwd[q], axes[1 - q], 1) for q in both]

    whole_width = rhs_two.shape[4]
    (early,) = couple(0, picked, factor, pieces + fwd, 0, whole_width, sends=False)
    early, send = couple(1, picked, factor, bwd, 0, whole_width, before=early)
    early_other = swap_cores(send)
    width = whole_width // PARTS
    solved_two = []
    for i in range(PARTS):
        start = i * width
        keep, send = couple(2, picked, factor, far, start, width)
        held, fwd, bwd = reduce_along_z(start, early, early_other, keep, swap_cores(send))
        kernel = functools.partial(last_kernel, start)
        solved_two = call(
            kernel, [shape((rows, start + width))], held, fwd, bwd, rhs_two[0, 0, 0], inv_two[0, 0, 0], *solved_two
        )
    return (solved_one[None, None], solved_two[0][None, None, None])


def solution(mesh):
    in_specs = (
        P("row", "col", None, None, None),
        P("row", "col", None, None, None),
        P("row", "col", None, None, None),
        P("row", "col", None, None, None),
        P("row", "col", None, None, None),
        P("row", "col", None),
        P("row", "col", None),
    )
    out_specs = (P("row", "col", None, None, None), P("row", "col", None, None, None))
    return jax.shard_map(local, mesh=mesh, in_specs=in_specs, out_specs=out_specs, check_vma=False)
```

```python
import functools

import jax
import jax.numpy as jnp
from jax import lax
from jax.experimental import pallas as pl
from jax.experimental.pallas import tpu as pltpu
from jax.sharding import PartitionSpec as P

PARTS = 2
STEP = 20
BOTH = ("row", "col")
MIB = 1024 * 1024
F32 = jnp.float32
BF16 = jnp.bfloat16


def whole(memory=pltpu.VMEM):
    return pl.BlockSpec(memory_space=memory)


def shape(dims, dtype=BF16):
    return jax.ShapeDtypeStruct(dims, dtype)


def params(mib=16):
    return pltpu.CompilerParams(vmem_limit_bytes=mib * MIB)


def ring_pairs(axis, steps):
    pairs = []
    for y in range(4):
        for x in range(4):
            for z in range(8):
                for core in range(2):
                    way = steps if core == 0 else -steps
                    to_y, to_x, to_z = y, x, z
                    if axis == "x":
                        to_x = (x + way) % 4
                    elif axis == "y":
                        to_y = (y + way) % 4
                    else:
                        to_z = (z + way) % 8
                    pairs.append(((y * 4 + x) * 16 + z * 2 + core, (to_y * 4 + to_x) * 16 + to_z * 2 + core))
    return pairs


def move(value, axis, steps):
    return lax.ppermute(value, BOTH, ring_pairs(axis, steps))


def swap_cores(value):
    return lax.ppermute(value, "col", [(i, i ^ 1) for i in range(16)])


def solve_one_kernel(rhs_hbm, inverse_hbm, solved, rhs, inverse, sems):
    copies = []
    for q in range(2):
        copies.append(pltpu.make_async_copy(rhs_hbm.at[q], rhs.at[q], sems.at[2 * q]))
        copies.append(pltpu.make_async_copy(inverse_hbm.at[q], inverse.at[q], sems.at[2 * q + 1]))
    for copy in copies:
        copy.start()
    for q in range(2):
        copies[2 * q].wait()
        copies[2 * q + 1].wait()
        solved[q] = jnp.dot(inverse[q], rhs[q], preferred_element_type=F32).astype(BF16)


def solve_one(rhs, inverse):
    return pl.pallas_call(
        solve_one_kernel,
        out_shape=shape(rhs.shape),
        in_specs=[whole(pltpu.HBM)] * 2,
        out_specs=whole(),
        scratch_shapes=[
            pltpu.VMEM(rhs.shape, BF16),
            pltpu.VMEM(inverse.shape, BF16),
            pltpu.SemaphoreType.DMA((4,)),
        ],
        compiler_params=params(),
    )(*[pltpu.with_memory_space_constraint(value, pltpu.HBM) for value in (rhs, inverse)])


def stage_kernel(blocks_hbm, first_line, second_line, blocks, first_same, second_same, sems):
    size = blocks.shape[0] // STEP
    copies = [
        pltpu.make_async_copy(first_line, first_same, sems.at[size]),
        pltpu.make_async_copy(second_line, second_same, sems.at[size + 1]),
    ]
    for i in range(size):
        span = pl.ds(i * STEP, STEP)
        copies.append(pltpu.make_async_copy(blocks_hbm.at[span], blocks.at[span], sems.at[i]))
    for copy in copies:
        copy.start()
    for copy in copies:
        copy.wait()


def stage(blocks, lines):
    return pl.pallas_call(
        stage_kernel,
        out_shape=[pltpu.VMEM(blocks.shape, blocks.dtype)] + [shape(line.shape) for line in lines],
        in_specs=[whole(pl.ANY)] * 3,
        out_specs=[whole()] + [whole(pl.ANY)] * 2,
        scratch_shapes=[pltpu.SemaphoreType.DMA((blocks.shape[0] // STEP + 2,))],
        compiler_params=params(4),
    )(pltpu.with_memory_space_constraint(blocks, pltpu.HBM), *lines)


def couple_kernel(turn, size, start, goes_on, sends, picked, blocks, *refs):
    pieces = refs[:size]
    refs = refs[size + goes_on :]
    total, sources, sems = refs[0], refs[-2], refs[-1]
    width = sources.shape[2]
    copies = []
    slot = 0
    for i, piece in enumerate(pieces):
        spot = sources.at[pl.ds(slot, piece.shape[0])]
        copies.append(pltpu.make_async_copy(piece.at[:, :, pl.ds(start, width)], spot, sems.at[i]))
        copies[-1].start()
        slot += piece.shape[0]
    if not goes_on:
        total[...] = jnp.zeros_like(total)
    for copy in copies:
        copy.wait()

    def products(group, carry):
        for j in range(STEP):
            entry = picked[turn, group * STEP + j]
            block, source, target = entry >> 11, (entry >> 5) & 63, 16 - (entry & 31)
            total[target] += jnp.dot(blocks[block], sources[source], preferred_element_type=F32)
        return carry

    def more(group):
        return (group < blocks.shape[0] // STEP) & (picked[turn, jnp.minimum(group * STEP, blocks.shape[0] - 1)] != 0)

    lax.while_loop(more, lambda group: products(group, group + 1), 0)
    if sends:
        refs[1][...] = total[8:16].astype(BF16)


def couple(turn, picked, blocks, pieces, start, width, before=None, sends=True):
    count, rows, _ = blocks.shape
    goes_on = before is not None
    in_vmem = [pltpu.with_memory_space_constraint(value, pltpu.VMEM) for value in ([blocks, before] if goes_on else [blocks])]
    return pl.pallas_call(
        functools.partial(couple_kernel, turn, len(pieces), start, int(goes_on), sends),
        out_shape=[pltpu.VMEM((17, rows, width), F32)] + [shape((8, rows, width))] * sends,
        in_specs=[whole(pltpu.SMEM)] + [whole()] + [whole(pl.ANY)] * len(pieces) + [whole()] * goes_on,
        out_specs=[whole()] * (1 + sends),
        scratch_shapes=[
            pltpu.VMEM((sum(piece.shape[0] for piece in pieces), rows, width), BF16),
            pltpu.SemaphoreType.DMA((len(pieces),)),
        ],
        input_output_aliases={2 + len(pieces): 0} if goes_on else {},
        compiler_params=params(16),
        cost_estimate=pl.CostEstimate(
            flops=2 * count * rows * rows * width, bytes_accessed=2 * count * rows * rows, transcendentals=0
        ),
    )(picked, in_vmem[0], *pieces, *in_vmem[1:])


def pick(turn, turns, source_slot, target_slot):
    size = turn.shape[0]
    index = jnp.arange(size, dtype=jnp.int32)
    wanted = turn[None, :] == jnp.arange(turns, dtype=jnp.int32)[:, None]
    before = index[None, :] < index[:, None]
    place = jnp.sum(wanted[:, None, :] & before[None], axis=2, dtype=jnp.int32)
    hits = wanted[:, None, :] & (place[:, None, :] == index[None, :, None])
    packed = (index * 64 + source_slot) * 32 + (16 - target_slot)
    return jnp.sum(jnp.where(hits, packed[None, None, :], 0), axis=2, dtype=jnp.int32)


ORDER = (4, 2, 5, 3, 6, 1, 7, 0)
PLACES = tuple(ORDER.index(u) for u in range(8))


def first_kernel(column, early, early_other, keep, other, fwd, bwd, held):
    def part(place):
        columns = slice(column, column + keep.shape[2])
        known = early[place, :, columns] + early_other[place, :, columns].astype(F32)
        return known + (keep[place] + other[place].astype(F32))

    fwd[0] = part(0).astype(BF16)
    fwd[1] = part(1).astype(BF16)
    bwd[...] = part(2).astype(BF16)
    for i in range(5):
        held[i] = part(3 + i)


def second_kernel(held, fwd, bwd, out_fwd, out_bwd):
    out_fwd[...] = (held[0] + fwd[0].astype(F32)).astype(BF16)
    out_bwd[...] = (held[1] + bwd[...].astype(F32)).astype(BF16)


def third_kernel(held, near, fwd, bwd, out_fwd, out_bwd):
    out_fwd[...] = (held[2] + (near[1].astype(F32) + fwd[...].astype(F32))).astype(BF16)
    out_bwd[...] = (held[3] + bwd[...].astype(F32)).astype(BF16)


def last_kernel(start, held, fwd, bwd, rhs, inverse, *refs):
    solved = refs[-1]
    width = held.shape[2]
    coupled = held[4] + (fwd[...].astype(F32) + bwd[...].astype(F32))
    residual = (rhs[:, start : start + width].astype(F32) - coupled).astype(BF16)
    value = jnp.dot(inverse[...], residual, preferred_element_type=F32).astype(BF16)
    if start:
        solved[:, :start] = refs[0][...]
    solved[:, start : start + width] = value


def call(kernel, outs, *args):
    return pl.pallas_call(
        kernel,
        out_shape=outs,
        in_specs=[whole()] * len(args),
        out_specs=[whole()] * len(outs),
        compiler_params=params(),
    )(*args)


def reduce_along_z(column, early, early_other, keep, other):
    _, rows, width = other.shape
    one = shape((rows, width))
    kernel = functools.partial(first_kernel, column)
    outs = [shape((2, rows, width)), one, shape((5, rows, width), F32)]
    fwd, bwd, held = call(kernel, outs, early, early_other, keep, other)
    near = move(fwd, "z", 1)
    bwd = move(bwd, "z", -1)
    fwd, bwd = call(second_kernel, [one, one], held, near, bwd)
    fwd = move(fwd, "z", 2)
    bwd = move(bwd, "z", -1)
    fwd, bwd = call(third_kernel, [one, one], held, near, fwd, bwd)
    return held, move(fwd, "z", 1), move(bwd, "z", -1)


def again_kernel(value, same, sem):
    copy = pltpu.make_async_copy(value, same, sem)
    copy.start()
    copy.wait()


def again(value):
    return pl.pallas_call(
        again_kernel,
        out_shape=shape(value.shape),
        in_specs=[whole(pl.ANY)],
        out_specs=whole(pl.ANY),
        scratch_shapes=[pltpu.SemaphoreType.DMA],
        compiler_params=params(1),
    )(value)


def local(rhs_one, inv_one, rhs_two, inv_two, blocks, block_rows, block_cols):
    rows = rhs_one.shape[3]
    row = lax.axis_index("row")
    col = lax.axis_index("col")
    core = col % 2
    sign = 1 - 2 * core
    here_y, here_x, here_z = row // 4, row % 4, col // 2

    target = block_rows[0, 0]
    parity = target % 2
    steps = ((1 - 2 * parity) * (target // 2 - here_z)) % 8
    target_slot = jnp.where(parity == core, 0, 8) + jnp.array(PLACES, jnp.int32)[steps]
    source = block_cols[0, 0]
    place = source // 2
    from_y = (sign * (place // 4 - here_y)) % 4
    from_x = (sign * (place % 4 - here_x)) % 4
    q = source % 2
    near = jnp.where(q == 0, from_x, from_y)
    distant = jnp.where(q == 0, from_y, from_x)
    first_phase = (near == 0) | (distant == 0)
    across = 3 * q + near - 1
    first_slot = jnp.where(from_y == 0, 2 * from_x, jnp.where(from_x == 0, 6 + 2 * from_y, 0)) + q
    turn = jnp.where(first_phase | (distant == 3), 0, distant)
    picked = pick(turn, 3, jnp.where(first_phase, first_slot, jnp.where(turn == 0, 14, 0) + across), target_slot)

    solved_one = solve_one(rhs_one[0, 0], inv_one[0, 0])
    axes = ("x", "y")
    both = range(2)
    fwd = [move(solved_one, axis, 1) for axis in axes]
    solved_later = again(solved_one)
    bwd = [move(solved_later, axis, -1) for axis in axes]
    far = [move(fwd[i], axes[i], 1) for i in both]
    pieces = [solved_one] + [piece for i in both for piece in (bwd[i], far[i], fwd[i])]

    lines = [jnp.concatenate([bwd[q][q : q + 1], far[q][q : q + 1], fwd[q][q : q + 1]]) for q in both]
    fwd = [move(lines[q], axes[1 - q], 1) for q in both]
    factor, *lines = stage(blocks[0, 0], lines)
    bwd = [move(lines[q], axes[1 - q], -1) for q in both]
    far = [move(fwd[q], axes[1 - q], 1) for q in both]

    whole_width = rhs_two.shape[4]
    (early,) = couple(0, picked, factor, pieces + fwd, 0, whole_width, sends=False)
    early, send = couple(1, picked, factor, bwd, 0, whole_width, before=early)
    early_other = swap_cores(send)
    width = whole_width // PARTS
    solved_two = []
    for i in range(PARTS):
        start = i * width
        keep, send = couple(2, picked, factor, far, start, width)
        held, fwd, bwd = reduce_along_z(start, early, early_other, keep, swap_cores(send))
        kernel = functools.partial(last_kernel, start)
        solved_two = call(
            kernel, [shape((rows, start + width))], held, fwd, bwd, rhs_two[0, 0, 0], inv_two[0, 0, 0], *solved_two
        )
    return (solved_one[None, None], solved_two[0][None, None, None])


def solution(mesh):
    in_specs = (
        P("row", "col", None, None, None),
        P("row", "col", None, None, None),
        P("row", "col", None, None, None),
        P("row", "col", None, None, None),
        P("row", "col", None, None, None),
        P("row", "col", None),
        P("row", "col", None),
    )
    out_specs = (P("row", "col", None, None, None), P("row", "col", None, None, None))
    return jax.shard_map(local, mesh=mesh, in_specs=in_specs, out_specs=out_specs, check_vma=False)
```
